256 devices in a mesh: row: 32 (over z, y_lo, core), col: 8 (over x, y_hi).
Axes of the slice: x: 4, y: 4 (y_hi: 2, y_lo: 2; y = y_hi * 2 + y_lo), z: 8, core: 2. Of those that a mesh axis runs over, the one named last changes fastest.
Arguments:
- homolog_stack: bfloat16 [256, 1024, 16], P(None, 'col'), may hold values from -6 to 6
- tensor_pairing_matrix: bfloat16 [256, 128], replicated, may hold values from -0.375 to 0.375
- stencil_filter_taps: bfloat16 [4, 2, 3, 3, 128, 128], replicated, may hold values from -0.1875 to 0.1875
- separation_class_matrix: bfloat16 [128, 64], replicated, may hold values from -0.5 to 0.5
- separation_class_offset: float32 [64], replicated, may hold values from -4 to 4
Outputs:
- distogram: bfloat16 [1024, 1024, 64], P('row', 'col')
The draws below stay inside these ranges and needn't reach their ends.
All inputs are finite; a program needn't handle non-finite values.
Results may differ from the reference program's by a relative error of at most 0.014.
Values may be sent and summed in bfloat16 or wider, within the bound.
A program may use at most 64 MiB of HBM per device.

```python
import jax
import jax.numpy as jnp
from jax import lax

HOMOLOG_TOTAL = 256
AMINO_TRAITS = 16
C = 128
BINS = 64
NB = 4
LOCAL_ROW_COUNT = 32
CHAIN_LENGTH = 1024
N_ROW = 32


def shard_levels(stream_key, shape, pieces, low, largest):
    level = 1.0
    for axis_at, shards_of in pieces:
        draws = jax.random.uniform(jax.random.fold_in(jax.random.fold_in(stream_key, 6), axis_at), (shards_of,), jnp.float32, low / len(pieces), largest / len(pieces))
        level = level * jnp.repeat(jnp.exp(draws), shape[axis_at] // shards_of).reshape((-1,) + (1,) * (len(shape) - 1 - axis_at))
    return level


def bell_draw(stream_key, dims, deviation, most, cuts=(), held_as=jnp.bfloat16):
    drawn = jax.random.normal(stream_key, dims, jnp.float32) * deviation
    if len(cuts) > 0:
        drawn = shard_levels(stream_key, dims, cuts, -0.22, 0.18) * drawn
    return jnp.clip(drawn, min=-most, max=most).astype(held_as)


def setup_inputs(seed: int = 0) -> dict:
    splits = jax.random.split(jax.random.key(seed), 6)
    homolog_stack = bell_draw(splits[0], (HOMOLOG_TOTAL, CHAIN_LENGTH, AMINO_TRAITS), 1.0, 6.0, ((1, 8),))
    tensor_pairing_matrix = bell_draw(splits[1], (AMINO_TRAITS * AMINO_TRAITS, C), (AMINO_TRAITS * AMINO_TRAITS) ** -0.5, 0.375)
    stencil_filter_taps = bell_draw(splits[2], (NB, 2, 3, 3, C, C), (9 * C) ** -0.5, 0.1875)
    separation_class_matrix = bell_draw(splits[3], (C, BINS), C ** -0.5, 0.5)
    separation_class_offset = bell_draw(splits[4], (BINS,), 1.0, 4.0, (), jnp.float32)
    return {"homolog_stack": homolog_stack, "tensor_pairing_matrix": tensor_pairing_matrix, "stencil_filter_taps": stencil_filter_taps, "separation_class_matrix": separation_class_matrix, "separation_class_offset": separation_class_offset}


def conv_full(h, weight, dilation):
    out = lax.conv_general_dilated(h.astype(jnp.float32)[None], weight.astype(jnp.float32), (1, 1), ((dilation, dilation), (dilation, dilation)), rhs_dilation=(dilation, dilation), dimension_numbers=('NHWC', 'HWIO', 'NHWC'), precision=lax.Precision.HIGHEST)
    return out[0]

def reference(homolog_stack, tensor_pairing_matrix, stencil_filter_taps, separation_class_matrix, separation_class_offset):
    homolog_padded_tile = homolog_stack.astype(jnp.float32)

    def pair_rows(row_begin_index):
        source_mapped_lines = lax.dynamic_slice_in_dim(homolog_padded_tile, row_begin_index, LOCAL_ROW_COUNT, 1)
        outer_product_pairs = jnp.einsum('uat,ugk->agtk', source_mapped_lines, homolog_padded_tile, precision=lax.Precision.HIGHEST) / HOMOLOG_TOTAL
        outer_product_pairs = outer_product_pairs.astype(jnp.bfloat16).reshape(LOCAL_ROW_COUNT * CHAIN_LENGTH, AMINO_TRAITS * AMINO_TRAITS)
        projected = jnp.dot(outer_product_pairs, tensor_pairing_matrix, preferred_element_type=jnp.float32)
        centre = projected - lax.optimization_barrier(jnp.mean(projected, axis=-1, keepdims=True))
        spread = lax.optimization_barrier(jnp.mean(centre * centre, axis=-1, keepdims=True))
        return (centre / jnp.sqrt(spread + 1e-05)).reshape(LOCAL_ROW_COUNT, CHAIN_LENGTH, C)
    starts = (jnp.arange(N_ROW, dtype=jnp.int32) * LOCAL_ROW_COUNT).astype(jnp.int32)
    state = lax.map(pair_rows, starts).reshape(CHAIN_LENGTH, CHAIN_LENGTH, C)
    for block in range(NB):
        dilation = 2 ** block
        first = jax.nn.elu(state).astype(jnp.bfloat16)
        second = jax.nn.elu(conv_full(first, stencil_filter_taps[block, 0], dilation)).astype(jnp.bfloat16)
        state = state + conv_full(second, stencil_filter_taps[block, 1], dilation)
    final = jax.nn.elu(state).astype(jnp.bfloat16).reshape(CHAIN_LENGTH * CHAIN_LENGTH, C)
    logits = jnp.dot(final, separation_class_matrix, preferred_element_type=jnp.float32) + separation_class_offset
    return logits.astype(jnp.bfloat16).reshape(CHAIN_LENGTH, CHAIN_LENGTH, BINS)
```

```python
import functools

import jax
import jax.numpy as jnp
from jax import lax
from jax.experimental import pallas as pl
from jax.experimental.pallas import tpu as pltpu
from jax.sharding import PartitionSpec as P

MESH = pl.DeviceIdType.MESH
F32, BF16 = jnp.float32, jnp.bfloat16

ROWS = 32
COLS = 128
HALO = 32
WIDE = COLS + 2 * HALO
TRAITS = 16
SEQS = 256
PIECE = 8
GROUP = 8
OFF = 4
XOFF = 2
TOP = 62
DEPTH = 74
PAD = 8

STAGES = (
    (1, 64, 8, 0, 192),
    (1, 64, 8, 0, 192),
    (2, 64, 8, 0, 192),
    (2, 56, 8, 0, 192),
    (4, 56, 8, 0, 192),
    (4, 48, 8, 0, 176),
    (8, 48, 16, 16, 160),
    (8, 32, 16, 16, 144),
)


def elu(v):
    return jnp.where(v > 0, v, jnp.exp(jnp.minimum(v, 0.0)) - 1.0)


def kernel(
    by_place,
    by_trait,
    pairing,
    taps,
    classes,
    offset,
    out,
    rows_got,
    cols_got,
    gram,
    weights,
    state,
    map_a,
    map_a_up,
    map_b,
    map_b_up,
    shift_in,
    shift_out,
    masks,
    centred,
    local_sem,
    scatter_send,
    scatter_recv,
    gather_send,
    gather_recv,
    edge_send,
    edge_recv,
    row_send,
    row_recv,
):
    r, c = lax.axis_index("row"), lax.axis_index("col")
    plane, y_lo, core = r // 4, (r // 2) % 2, r % 2
    partner = (r + 1 - 2 * core, c)

    barrier = pltpu.get_barrier_semaphore()
    for step in range(1, GROUP):
        pl.semaphore_signal(
            barrier, inc=1, device_id=(r, lax.rem(c + step, GROUP)), device_id_type=MESH
        )
    pl.semaphore_signal(barrier, inc=1, device_id=partner, device_id_type=MESH)
    pl.semaphore_wait(barrier, GROUP)

    first = -HALO + 64 * (y_lo + core)

    def source_of(piece):
        start = first + PIECE * piece + COLS
        return lax.rem(plane + start // COLS - 1 + GROUP, GROUP), lax.rem(start, COLS)

    def scatter_copy(piece):
        _, start = source_of(piece)
        return pltpu.make_async_remote_copy(
            src_ref=by_place.at[pl.ds(start, PIECE)],
            dst_ref=rows_got.at[pl.ds(PIECE * piece, PIECE)],
            send_sem=scatter_send.at[piece],
            recv_sem=scatter_recv,
            device_id=(r, piece),
            device_id_type=MESH,
        )

    own_source, own_start = source_of(c)
    own_slot = rows_got.at[pl.ds(PIECE * c, PIECE)]
    own_copy = pltpu.make_async_copy(
        by_place.at[pl.ds(own_start, PIECE)], own_slot, local_sem.at[0]
    )
    for piece in range(GROUP):
        source, _ = source_of(piece)

        @pl.when(jnp.logical_and(source == c, piece != c))
        def _():
            scatter_copy(piece).start()

    @pl.when(own_source == c)
    def _():
        own_copy.start()

    mine_cols = pltpu.make_async_copy(
        by_trait, cols_got.at[:, pl.ds(HALO, COLS)], local_sem.at[1]
    )
    mine_cols.start()
    side = pl.multiple_of((HALO + COLS) * core, HALO)
    edge_copy = pltpu.make_async_remote_copy(
        src_ref=by_trait.at[:, pl.ds(pl.multiple_of((COLS - HALO) * (1 - core), HALO), HALO)],
        dst_ref=cols_got.at[:, pl.ds(side, HALO)],
        send_sem=edge_send.at[0],
        recv_sem=edge_recv.at[0],
        device_id=(r, lax.rem(c + 1 - 2 * core + GROUP, GROUP)),
        device_id_type=MESH,
    )
    edge_copy.start()

    @pl.when(own_source == c)
    def _():
        own_copy.wait()

    @pl.when(own_source != c)
    def _():
        pltpu.make_async_remote_copy(
            src_ref=by_place.at[pl.ds(0, PIECE)],
            dst_ref=own_slot,
            send_sem=scatter_send.at[0],
            recv_sem=scatter_recv,
            device_id=(r, lax.rem(c + 1, GROUP)),
            device_id_type=MESH,
        ).wait_recv()

    def gather_copy(step):
        return pltpu.make_async_remote_copy(
            src_ref=own_slot,
            dst_ref=own_slot,
            send_sem=gather_send.at[step],
            recv_sem=gather_recv.at[step],
            device_id=(r, lax.rem(c + step, GROUP)),
            device_id_type=MESH,
        )

    for step in range(1, GROUP):
        gather_copy(step).start()
    edge_copy.wait_recv()
    other_copy = pltpu.make_async_remote_copy(
        src_ref=cols_got.at[:, pl.ds(side, HALO)],
        dst_ref=cols_got.at[:, pl.ds(side, HALO)],
        send_sem=edge_send.at[1],
        recv_sem=edge_recv.at[1],
        device_id=partner,
        device_id_type=MESH,
    )
    other_copy.start()

    def prepare(conv, carry):
        for q in range(3):
            g0 = taps[conv, 0, q].astype(F32)
            g1 = taps[conv, 1, q].astype(F32)
            g2 = taps[conv, 2, q].astype(F32)
            outer, inner = (g0 + g2) * 0.5, g1 * 0.5
            at = (pl.ds(128 * (q // 2), 128), pl.ds(128 * (1 if q == 0 else 0), 128))
            for m, v in enumerate((g0, outer + inner, outer - inner, g2)):
                weights[conv, m, at[0], at[1]] = v.astype(BF16)
        for m in range(4):
            weights[conv, m, 128:, 128:] = jnp.zeros((128, 128), BF16)
        return carry

    lax.fori_loop(0, 8, prepare, 0)
    full = pairing[...].astype(F32)
    centred[...] = (full - jnp.mean(full, axis=-1, keepdims=True)).astype(BF16)
    place = lax.broadcasted_iota(jnp.int32, (WIDE, 128), 0) + (c * COLS - HALO)
    inside = jnp.logical_and(place >= 0, place < COLS * GROUP)
    masks[0] = jnp.zeros((WIDE, 128), F32)
    masks[1] = jnp.where(inside, 1.0, 0.0).astype(F32)
    edge_row = jnp.where(jnp.logical_or(r == 0, r == 31), 30, -DEPTH)

    def mask_of(row):
        return masks[jnp.where(row < edge_row, 0, 1)]

    for ref in (map_a, map_a_up, map_b, map_b_up):
        ref[0:OFF] = jnp.zeros((OFF, WIDE, 128), BF16)
    shift_in[...] = jnp.zeros(shift_in.shape, F32)
    shift_out[...] = jnp.zeros(shift_out.shape, F32)

    mine_cols.wait()
    other_copy.wait()
    edge_copy.wait_send()
    for step in range(1, GROUP):
        pltpu.make_async_remote_copy(
            src_ref=own_slot,
            dst_ref=rows_got.at[pl.ds(PIECE * lax.rem(c - step + GROUP, GROUP), PIECE)],
            send_sem=gather_send.at[step],
            recv_sem=gather_recv.at[step],
            device_id=(r, lax.rem(c + step, GROUP)),
            device_id_type=MESH,
        ).wait()
    for piece in range(GROUP):
        source, _ = source_of(piece)

        @pl.when(jnp.logical_and(source == c, piece != c))
        def _():
            scatter_copy(piece).wait_send()

    def outer_product(b, carry):
        block = lax.dot_general(
            rows_got[...].reshape(64 * TRAITS, SEQS),
            cols_got[b],
            (((1,), (1,)), ((), ())),
            preferred_element_type=F32,
        )
        gram[:, pl.ds(pl.multiple_of(b * TRAITS, TRAITS), TRAITS), :] = (
            (block * (1.0 / SEQS)).astype(BF16).reshape(64, TRAITS, WIDE)
        )
        return carry

    lax.fori_loop(0, TRAITS, outer_product, 0)

    def put(value, row, slot, first_col, width, ahead, target, target_up):
        e = elu(value) * mask_of(row)[first_col : first_col + width]
        target[row + OFF, first_col : first_col + width] = e.astype(BF16)
        shift_out[slot, 0:width] = e
        target_up[row + OFF, first_col : first_col + width] = shift_out[
            slot, ahead : ahead + width
        ].astype(BF16)

    def row_copies(stage, count, target, target_up):
        return [
            pltpu.make_async_remote_copy(
                src_ref=ref.at[TOP - 1 - t + OFF],
                dst_ref=ref.at[TOP + t + OFF],
                send_sem=row_send.at[stage % 2, which, t],
                recv_sem=row_recv.at[stage % 2, which, t],
                device_id=partner,
                device_id_type=MESH,
            )
            for t in range(count)
            for which, ref in enumerate((target, target_up))
        ]

    def start_all(copies):
        for copy in copies:
            copy.start()

    def wait_all(copies):
        for copy in copies:
            copy.wait()

    def first_rows(chunk, carry):
        for slot in range(2):
            row = TOP - 1 - 2 * chunk - slot
            got = row + 2 + core * (59 - 2 * row)
            projected = lax.dot_general(
                gram[got],
                centred[...],
                (((0,), (0,)), ((), ())),
                preferred_element_type=F32,
            )
            spread = jnp.mean(projected * projected, axis=-1, keepdims=True)
            value = projected * lax.rsqrt(spread + 1e-05)
            state[row + XOFF] = value
            put(value, row, slot, 0, WIDE, 1, map_a, map_a_up)
        return carry

    first_rows(0, 0)
    copies = row_copies(0, 1, map_a, map_a_up)
    start_all(copies)
    lax.fori_loop(1, TOP // 2, first_rows, 0)

    for stage, (d, rows, depth, col, width) in enumerate(STAGES):
        source, source_up = (map_a, map_a_up) if stage % 2 == 0 else (map_b, map_b_up)
        target, target_up = (map_b, map_b_up) if stage % 2 == 0 else (map_a, map_a_up)
        residual, last = stage % 2 == 1, stage == 7
        ahead = 0 if last else STAGES[stage + 1][0]
        pairs = depth // 2
        wait_all(copies)

        def chunk_of(
            chunk,
            carry,
            stage=stage,
            d=d,
            depth=depth,
            col=col,
            width=width,
            source=source,
            source_up=source_up,
            target=target,
            target_up=target_up,
            residual=residual,
            last=last,
            ahead=ahead,
            pairs=pairs,
        ):
            base = TOP - depth * (chunk + 1)
            span = slice(col, col + width)

            def lines(ref, at):
                parts = [
                    ref[pl.ds(base + OFF + 2 * d * k + at, d), span]
                    for k in range(depth // (2 * d))
                ]
                return parts[0] if len(parts) == 1 else jnp.concatenate(parts, axis=0)

            sides = []
            for ref in (source, source_up):
                d0, d1, d2, d3 = (lines(ref, (k - 1) * d) for k in range(4))
                sides.append((d0 - d2, d1 + d2, d2 - d1, d1 - d3))
            products = []
            for m in range(4):
                both = jnp.concatenate((sides[0][m], sides[1][m]), axis=-1)
                tap = m if m in (1, 2) else (3 * core if m == 0 else 3 - 3 * core)
                products.append(
                    jnp.dot(
                        both.reshape(pairs * width, 256),
                        weights[stage, tap],
                        preferred_element_type=F32,
                    )
                )
            m0, m1, m2, m3 = products
            upper = (m0 + m1 + m2).reshape(pairs, width, 256)
            lower = (m1 - m2 - m3).reshape(pairs, width, 256)
            for p in range(pairs):
                block, t = p // d, p % d
                for half, value in enumerate((upper, lower)):
                    slot = 2 * p + half
                    row = base + 2 * d * block + d * half + t
                    shift_in[slot, PAD : PAD + width] = value[p, :, 128:]
                    conv = value[p, :, :128] + shift_in[slot, PAD - d : PAD - d + width]
                    if residual:
                        conv = conv + state[row + XOFF, span]
                        if not last:
                            state[row + XOFF, span] = conv
                    if last:
                        final = elu(conv[16:144]).astype(BF16)
                        logits = lax.dot_general(
                            classes[...],
                            final,
                            (((1,), (1,)), ((), ())),
                            preferred_element_type=F32,
                        )
                        own = row - 30
                        out[own + core * (31 - 2 * own)] = (logits + offset[...]).astype(BF16)
                    else:
                        put(conv, row, slot, col, width, ahead, target, target_up)
            return carry

        chunk_of(0, 0)
        if not last:
            copies = row_copies(stage + 1, ahead, target, target_up)
            start_all(copies)
        lax.fori_loop(1, rows // depth, chunk_of, 0)


def body(homologs, pairing, taps, classes, offset):
    by_place = jnp.transpose(homologs, (1, 2, 0))
    by_trait = jnp.transpose(homologs, (2, 1, 0))
    pairing = pairing.reshape(TRAITS, TRAITS, 128).transpose(1, 0, 2).reshape(256, 128)
    taps = taps.reshape(8, 3, 3, 128, 128)
    vmem = pl.BlockSpec(memory_space=pltpu.VMEM)
    out = pl.pallas_call(
        kernel,
        out_shape=jax.ShapeDtypeStruct((ROWS, 64, COLS), BF16),
        in_specs=[vmem] * 6,
        out_specs=vmem,
        scratch_shapes=[
            pltpu.VMEM((64, TRAITS, SEQS), BF16),
            pltpu.VMEM((TRAITS, WIDE, SEQS), BF16),
            pltpu.VMEM((64, TRAITS * TRAITS, WIDE), BF16),
            pltpu.VMEM((8, 4, 256, 256), BF16),
            pltpu.VMEM((64, WIDE, 128), F32),
            pltpu.VMEM((DEPTH, WIDE, 128), BF16),
            pltpu.VMEM((DEPTH, WIDE, 128), BF16),
            pltpu.VMEM((DEPTH, WIDE, 128), BF16),
            pltpu.VMEM((DEPTH, WIDE, 128), BF16),
            pltpu.VMEM((16, PAD + WIDE, 128), F32),
            pltpu.VMEM((16, WIDE + PAD, 128), F32),
            pltpu.VMEM((2, WIDE, 128), F32),
            pltpu.VMEM((256, 128), BF16),
            pltpu.SemaphoreType.DMA((2,)),
            pltpu.SemaphoreType.DMA((GROUP,)),
            pltpu.SemaphoreType.DMA,
            pltpu.SemaphoreType.DMA((GROUP,)),
            pltpu.SemaphoreType.DMA((GROUP,)),
            pltpu.SemaphoreType.DMA((2,)),
            pltpu.SemaphoreType.DMA((2,)),
            pltpu.SemaphoreType.DMA((2, 2, 8)),
            pltpu.SemaphoreType.DMA((2, 2, 8)),
        ],
        compiler_params=pltpu.CompilerParams(
            collective_id=0, has_side_effects=True, vmem_limit_bytes=60 * 2**20
        ),
        name="distogram",
    )(by_place, by_trait, pairing, taps, classes.T, offset.reshape(64, 1))
    return jnp.transpose(out, (0, 2, 1))


def solution(mesh):
    placed = (P(None, "col", None), P(), P(), P(), P())
    return jax.shard_map(
        body, mesh=mesh, in_specs=placed, out_specs=P("row", "col", None), check_vma=False
    )
```

```python
import functools

import jax
import jax.numpy as jnp
from jax import lax
from jax.experimental import pallas as pl
from jax.experimental.pallas import tpu as pltpu
from jax.sharding import PartitionSpec as P

MESH = pl.DeviceIdType.MESH
F32, BF16 = jnp.float32, jnp.bfloat16

ROWS = 32
COLS = 128
HALO = 32
WIDE = COLS + 2 * HALO
TRAITS = 16
SEQS = 256
PIECE = 16
HALF = TRAITS // 2
GROUP = 8
OFF = 4
XOFF = 2
TOP = 62
DEPTH = 74
PAD = 8

STAGES = (
    (1, (16, 16, 16, 14), 0, 192),
    (1, (16, 16, 16, 12), 0, 192),
    (2, (16, 16, 16, 12), 0, 192),
    (2, (16, 16, 12, 12), 0, 192),
    (4, (16, 16, 16, 8), 0, 192),
    (4, (16, 16, 16), 0, 176),
    (8, (16, 16, 16), 16, 160),
    (8, (16, 16), 16, 144),
)


def elu(v):
    return jnp.maximum(v, jnp.exp(jnp.minimum(v, 0.0)) - 1.0)


def kernel(
    homologs,
    pairing,
    taps_far,
    classes,
    offset,
    out,
    staged,
    rows_got,
    rows_in,
    cols_got,
    gram,
    weights,
    state,
    map_a,
    map_a_up,
    map_b,
    map_b_up,
    products_a,
    products_b,
    shift_out,
    masks,
    taps,
    centred,
    local_sem,
    scatter_send,
    scatter_recv,
    gather_send,
    gather_recv,
    edge_send,
    edge_recv,
    row_send,
    row_recv,
):
    r, c = lax.axis_index("row"), lax.axis_index("col")
    plane, y_lo, core = r // 4, (r // 2) % 2, r % 2
    partner = (r + 1 - 2 * core, c)

    across = r + 2 - 4 * y_lo
    edge_to = (across, lax.rem(c + 1 - 2 * core + GROUP, GROUP))
    edge_from = (across, lax.rem(c - 1 + 2 * core + GROUP, GROUP))

    barrier = pltpu.get_barrier_semaphore()
    peers = [(r, lax.rem(c + step, GROUP)) for step in range(1, GROUP)]
    peers += [partner, edge_to, edge_from]
    for peer in peers:
        pl.semaphore_signal(barrier, inc=1, device_id=peer, device_id_type=MESH)
    taps_copy = pltpu.make_async_copy(taps_far, taps, local_sem.at[1])
    taps_copy.start()

    def widen(k, carry):
        at = pl.multiple_of(k * 16, 16)
        staged[pl.ds(pl.multiple_of(k * 256, 256), 256)] = (
            homologs[pl.ds(at, 16)].astype(F32).reshape(256, 128)
        )
        return carry

    lax.fori_loop(0, 16, widen, 0)

    def turn(k, carry):
        for a in range(2):
            trait = 2 * k + a
            flat = staged[pl.ds(trait, SEQS, stride=TRAITS)]
            cols_got[trait, HALO : HALO + COLS] = flat.T.astype(BF16)
        return carry

    lax.fori_loop(0, TRAITS // 2, turn, 0)
    pl.semaphore_wait(barrier, len(peers))

    first = -HALO + 64 * (y_lo + core)

    def source_of(piece):
        start = first + PIECE * (piece // 2) + COLS
        return lax.rem(plane + start // COLS - 1 + GROUP, GROUP), lax.rem(start, COLS)

    def piece_at(piece):
        _, start = source_of(piece)
        return cols_got.at[
            pl.ds(HALF * (piece % 2), HALF), pl.ds(pl.multiple_of(HALO + start, PIECE), PIECE)
        ]

    def slot_of(piece):
        return rows_got.at[
            pl.ds(HALF * (piece % 2), HALF),
            pl.ds(pl.multiple_of(PIECE * (piece // 2), PIECE), PIECE),
        ]

    def scatter_copy(piece):
        return pltpu.make_async_remote_copy(
            src_ref=piece_at(piece),
            dst_ref=slot_of(piece),
            send_sem=scatter_send.at[piece],
            recv_sem=scatter_recv,
            device_id=(r, piece),
            device_id_type=MESH,
        )

    own_source, _ = source_of(c)
    own_slot = slot_of(c)
    own_copy = pltpu.make_async_copy(piece_at(c), own_slot, local_sem.at[0])
    for piece in range(GROUP):
        source, _ = source_of(piece)

        @pl.when(jnp.logical_and(source == c, piece != c))
        def _():
            scatter_copy(piece).start()

    @pl.when(own_source == c)
    def _():
        own_copy.start()

    side = pl.multiple_of((HALO + COLS) * core, HALO)
    edge_copy = pltpu.make_async_remote_copy(
        src_ref=cols_got.at[:, pl.ds(pl.multiple_of(COLS - (COLS - HALO) * core, HALO), HALO)],
        dst_ref=cols_got.at[:, pl.ds(side, HALO)],
        send_sem=edge_send.at[0],
        recv_sem=edge_recv.at[0],
        device_id=edge_to,
        device_id_type=MESH,
    )
    edge_copy.start()

    @pl.when(own_source == c)
    def _():
        own_copy.wait()

    @pl.when(own_source != c)
    def _():
        pltpu.make_async_remote_copy(
            src_ref=own_slot,
            dst_ref=own_slot,
            send_sem=scatter_send.at[0],
            recv_sem=scatter_recv,
            device_id=(r, lax.rem(c + 1, GROUP)),
            device_id_type=MESH,
        ).wait_recv()

    def gather_copy(step, place):
        return pltpu.make_async_remote_copy(
            src_ref=own_slot,
            dst_ref=place,
            send_sem=gather_send.at[step],
            recv_sem=gather_recv.at[step],
            device_id=(r, lax.rem(c + step, GROUP)),
            device_id_type=MESH,
        )

    for step in range(1, GROUP):
        gather_copy(step, own_slot).start()
    edge_copy.wait_recv()
    other_copy = pltpu.make_async_remote_copy(
        src_ref=cols_got.at[:, pl.ds(side, HALO)],
        dst_ref=cols_got.at[:, pl.ds(side, HALO)],
        send_sem=edge_send.at[1],
        recv_sem=edge_recv.at[1],
        device_id=partner,
        device_id_type=MESH,
    )
    other_copy.start()

    def prepare(conv, carry):
        for q in range(3):
            g0 = taps[conv, 0, q].astype(F32)
            g1 = taps[conv, 1, q].astype(F32)
            g2 = taps[conv, 2, q].astype(F32)
            outer, inner = (g0 + g2) * 0.5, g1 * 0.5
            at = (pl.ds(128 * (q // 2), 128), pl.ds(128 * (1 if q == 0 else 0), 128))
            for m, v in enumerate((g0, outer + inner, outer - inner, g2)):
                weights[conv, m, at[0], at[1]] = v.astype(BF16)
        for m in range(4):
            weights[conv, m, 128:, 128:] = jnp.zeros((128, 128), BF16)
        return carry

    taps_copy.wait()
    lax.fori_loop(0, 8, prepare, 0)
    full = pairing[...].astype(F32)
    full = (full - jnp.mean(full, axis=-1, keepdims=True)).astype(BF16)
    to = lax.broadcasted_iota(jnp.int32, (256, 256), 0)
    at = lax.broadcasted_iota(jnp.int32, (256, 256), 1)
    order = jnp.where(at == lax.rem(to, TRAITS) * TRAITS + to // TRAITS, 1.0, 0.0).astype(BF16)
    centred[...] = jnp.dot(order, full, preferred_element_type=F32).astype(BF16)
    same = lax.broadcasted_iota(jnp.int32, (64, 64), 0) == lax.broadcasted_iota(
        jnp.int32, (64, 64), 1
    )
    bias = jnp.sum(jnp.where(same, offset[...], 0.0), axis=1, keepdims=True)
    place = lax.broadcasted_iota(jnp.int32, (WIDE, 128), 0) + (c * COLS - HALO)
    inside = jnp.logical_and(place >= 0, place < COLS * GROUP)
    masks[0] = jnp.zeros((WIDE, 128), F32)
    masks[1] = jnp.where(inside, 1.0, 0.0).astype(F32)
    edge_row = jnp.where(jnp.logical_or(r == 0, r == 31), 30, -DEPTH)

    def mask_of(row):
        return masks[jnp.where(row < edge_row, 0, 1)]

    for ref in (map_a, map_a_up, map_b, map_b_up):
        ref[0:OFF] = jnp.zeros((OFF, WIDE, 128), BF16)
    for ref in (products_a, products_b):
        ref[:, :, 0:PAD] = jnp.zeros((4, 2, PAD, 128), F32)
    shift_out[...] = jnp.zeros(shift_out.shape, F32)

    other_copy.wait()
    edge_copy.wait_send()
    for step in range(1, GROUP):
        gather_copy(step, slot_of(lax.rem(c - step + GROUP, GROUP))).wait()
    for piece in range(GROUP):
        source, _ = source_of(piece)

        @pl.when(jnp.logical_and(source == c, piece != c))
        def _():
            scatter_copy(piece).wait_send()

    for a in range(TRAITS):
        for k in range(2):
            staged[pl.ds(1024 * k + a, 64, stride=TRAITS)] = rows_got[
                a, :, 128 * k : 128 * (k + 1)
            ].astype(F32)
    for k in range(2):
        rows_in[:, 128 * k : 128 * (k + 1)] = staged[1024 * k : 1024 * (k + 1)].astype(BF16)

    def outer_product(group, carry):
        for k in range(4):
            b = 4 * group + k
            block = lax.dot_general(
                rows_in[...],
                cols_got[b],
                (((1,), (1,)), ((), ())),
                preferred_element_type=F32,
            )
            gram[:, pl.ds(pl.multiple_of(b * TRAITS, TRAITS), TRAITS), :] = (
                (block * (1.0 / SEQS)).astype(BF16).reshape(64, TRAITS, WIDE)
            )
        return carry

    lax.fori_loop(0, TRAITS // 4, outer_product, 0)

    def put(value, row, slot, first_col, width, ahead, target, target_up, whole):
        e = elu(value)
        low, high = HALO - first_col, HALO + COLS - first_col
        if whole:
            e = e * mask_of(row)[first_col : first_col + width]
        else:
            parts = [e[:low] * masks[1, first_col:HALO], e[low : min(high, width)]]
            if width > high:
                parts.append(e[high:] * masks[1, HALO + COLS : first_col + width])
            e = jnp.concatenate(parts, axis=0)
        target[row + OFF, first_col : first_col + width] = e.astype(BF16)
        if ahead == 8:
            moved = jnp.concatenate((e[8:], e[:8]), axis=0)
        else:
            shift_out[slot, 0:width] = e
            moved = shift_out[slot, ahead : ahead + width]
        target_up[row + OFF, first_col : first_col + width] = moved.astype(BF16)

    def row_copies(stage, count, target, target_up):
        return [
            pltpu.make_async_remote_copy(
                src_ref=ref.at[TOP - 1 - t + OFF],
                dst_ref=ref.at[TOP + t + OFF],
                send_sem=row_send.at[stage % 2, which, t],
                recv_sem=row_recv.at[stage % 2, which, t],
                device_id=partner,
                device_id_type=MESH,
            )
            for t in range(count)
            for which, ref in enumerate((target, target_up))
        ]

    def start_all(copies):
        for copy in copies:
            copy.start()

    def wait_all(copies):
        for copy in copies:
            copy.wait()

    def first_rows(chunk, carry):
        for slot in range(8):
            row = TOP - 1 - 8 * chunk - slot
            got = row + 2 + core * (59 - 2 * row)
            projected = lax.dot_general(
                gram[got],
                centred[...],
                (((0,), (0,)), ((), ())),
                preferred_element_type=F32,
            )
            spread = jnp.mean(projected * projected, axis=-1, keepdims=True)
            value = projected * lax.rsqrt(spread + 1e-05)
            state[row + XOFF] = value
            put(value, row, slot, 0, WIDE, 1, map_a, map_a_up, True)
        return carry

    first_rows(0, 0)
    copies = row_copies(0, 1, map_a, map_a_up)
    start_all(copies)
    lax.fori_loop(1, 8, first_rows, 0)

    def maps_of(stage):
        pair = ((map_a, map_a_up), (map_b, map_b_up))
        return pair[stage % 2], pair[1 - stage % 2]

    def multiply(item, m, held):
        stage, base, depth = item
        d, _, col, width = STAGES[stage]
        span = slice(col, col + width)
        low, high, sign = ((0, 2, -1), (1, 2, 1), (2, 1, -1), (1, 3, -1))[m]

        def lines(ref, at):
            parts = [
                ref[base + OFF + 2 * d * k + at : base + OFF + 2 * d * k + at + d, span]
                for k in range(depth // (2 * d))
            ]
            return parts[0] if len(parts) == 1 else jnp.concatenate(parts, axis=0)

        sides = []
        for ref in maps_of(stage)[0]:
            x, y = lines(ref, (low - 1) * d), lines(ref, (high - 1) * d)
            sides.append(x + y if sign > 0 else x - y)
        count = depth // 2 * width
        tap = m if m in (1, 2) else (3 * core if m == 0 else 3 - 3 * core)
        product = jnp.dot(
            jnp.concatenate(sides, axis=-1).reshape(count, 256),
            weights[stage, tap],
            preferred_element_type=F32,
        )
        held[m, 0, PAD : PAD + count] = product[:, :128]
        held[m, 1, PAD : PAD + count] = product[:, 128:]

    def finish(item, pairs, held):
        stage, base, depth = item
        d, _, col, width = STAGES[stage]
        residual, last = stage % 2 == 1, stage == len(STAGES) - 1
        target, target_up = maps_of(stage)[1]
        span = slice(col, col + width)
        for p in pairs:
            block, t = p // d, p % d
            at = PAD + p * width

            def term(m, at=at):
                return held[m, 0, at : at + width], held[m, 1, at - d : at - d + width]

            (a0, b0), (a1, b1), (a2, b2), (a3, b3) = (term(m) for m in range(4))
            upper = (a0 + b0) + (a1 + b1) + (a2 + b2)
            lower = (a1 + b1) - (a2 + b2) - (a3 + b3)
            for half, conv in enumerate((upper, lower)):
                row = base + 2 * d * block + d * half + t
                if residual:
                    conv = conv + state[row + XOFF, span]
                    if not last:
                        state[row + XOFF, span] = conv
                if last:
                    final = elu(conv[16:144]).astype(BF16)
                    logits = lax.dot_general(
                        classes[...],
                        final,
                        (((1,), (1,)), ((), ())),
                        preferred_element_type=F32,
                    )
                    own = row - 30
                    out[own + core * (31 - 2 * own)] = (logits + bias).astype(BF16)
                else:
                    ahead = STAGES[stage + 1][0]
                    slot = 2 * p + half
                    put(conv, row, slot, col, width, ahead, target, target_up, row < 30)

    items = []
    for stage, (_, depths, _, _) in enumerate(STAGES):
        base = TOP
        for depth in depths:
            base -= depth
            items.append((stage, base, depth))

    done, held_done = None, None
    for step, item in enumerate(items + [None]):
        held = (products_a, products_b)[step % 2]
        if item is not None and item[1] + item[2] == TOP:
            wait_all(copies)
        for m in range(4):
            if item is not None:
                multiply(item, m, held)
            if done is not None:
                pairs = done[2] // 2
                finish(done, range(pairs * m // 4, pairs * (m + 1) // 4), held_done)
        if done is not None and done[1] + done[2] == TOP and done[0] + 1 < len(STAGES):
            copies = row_copies(done[0] + 1, STAGES[done[0] + 1][0], *maps_of(done[0])[1])
            start_all(copies)
        done, held_done = item, held


def body(homologs, pairing, taps, classes, offset):
    homologs = jnp.transpose(homologs, (0, 2, 1))
    taps = taps.reshape(8, 3, 3, 128, 128)
    vmem = pl.BlockSpec(memory_space=pltpu.VMEM)
    far = pl.BlockSpec(memory_space=pl.ANY)
    out = pl.pallas_call(
        kernel,
        out_shape=jax.ShapeDtypeStruct((ROWS, 64, COLS), BF16),
        in_specs=[vmem, vmem, far, vmem, vmem],
        out_specs=vmem,
        scratch_shapes=[
            pltpu.VMEM((SEQS * TRAITS, 128), F32),
            pltpu.VMEM((TRAITS, 64, SEQS), BF16),
            pltpu.VMEM((64 * TRAITS, SEQS), BF16),
            pltpu.VMEM((TRAITS, WIDE, SEQS), BF16),
            pltpu.VMEM((64, TRAITS * TRAITS, WIDE), BF16),
            pltpu.VMEM((8, 4, 256, 256), BF16),
            pltpu.VMEM((64, WIDE, 128), F32),
            pltpu.VMEM((DEPTH, WIDE, 128), BF16),
            pltpu.VMEM((DEPTH, WIDE, 128), BF16),
            pltpu.VMEM((DEPTH, WIDE, 128), BF16),
            pltpu.VMEM((DEPTH, WIDE, 128), BF16),
            pltpu.VMEM((4, 2, PAD + 8 * WIDE, 128), F32),
            pltpu.VMEM((4, 2, PAD + 8 * WIDE, 128), F32),
            pltpu.VMEM((16, WIDE + PAD, 128), F32),
            pltpu.VMEM((2, WIDE, 128), F32),
            pltpu.VMEM((8, 3, 3, 128, 128), BF16),
            pltpu.VMEM((256, 128), BF16),
            pltpu.SemaphoreType.DMA((2,)),
            pltpu.SemaphoreType.DMA((GROUP,)),
            pltpu.SemaphoreType.DMA,
            pltpu.SemaphoreType.DMA((GROUP,)),
            pltpu.SemaphoreType.DMA((GROUP,)),
            pltpu.SemaphoreType.DMA((2,)),
            pltpu.SemaphoreType.DMA((2,)),
            pltpu.SemaphoreType.DMA((2, 2, 8)),
            pltpu.SemaphoreType.DMA((2, 2, 8)),
        ],
        compiler_params=pltpu.CompilerParams(
            collective_id=0, has_side_effects=True, vmem_limit_bytes=60 * 2**20
        ),
        name="distogram",
    )(homologs, pairing, taps, classes.T, offset.reshape(1, 64))
    return jnp.transpose(out, (0, 2, 1))


def solution(mesh):
    placed = (P(None, "col", None), P(), P(), P(), P())
    return jax.shard_map(
        body, mesh=mesh, in_specs=placed, out_specs=P("row", "col", None), check_vma=False
    )
```

```python
import functools

import jax
import jax.numpy as jnp
from jax import lax
from jax.experimental import pallas as pl
from jax.experimental.pallas import tpu as pltpu
from jax.sharding import PartitionSpec as P

MESH = pl.DeviceIdType.MESH
F32, BF16 = jnp.float32, jnp.bfloat16

ROWS = 32
COLS = 128
HALO = 32
WIDE = COLS + 2 * HALO
TRAITS = 16
SEQS = 256
BLOCK = 16
BLOCKS = 4
SHARE = 2
GROUP = 8
OFF = 4
XOFF = 2
TOP = 62
DEPTH = 74
PAD = 8

STAGES = (
    (1, (16, 16, 16, 14), 0, 192),
    (1, (16, 16, 16, 12), 0, 192),
    (2, (16, 16, 16, 12), 0, 192),
    (2, (16, 16, 12, 12), 0, 192),
    (4, (16, 16, 16, 8), 0, 192),
    (4, (16, 16, 16), 0, 176),
    (8, (16, 16, 16), 16, 160),
    (8, (16, 16), 16, 144),
)


def elu(v):
    return jnp.maximum(v, jnp.exp(jnp.minimum(v, 0.0)) - 1.0)


def kernel(
    homologs,
    pairing,
    taps_far,
    classes,
    offset,
    out,
    staged,
    rows_got,
    rows_in,
    cols_got,
    gram,
    weights,
    state,
    map_a,
    map_a_up,
    map_b,
    map_b_up,
    products_a,
    products_b,
    shift_out,
    masks,
    taps,
    centred,
    local_sem,
    scatter_send,
    scatter_recv,
    gather_send,
    gather_recv,
    edge_send,
    edge_recv,
    row_send,
    row_recv,
):
    r, c = lax.axis_index("row"), lax.axis_index("col")
    plane, y_lo, core = r // 4, (r // 2) % 2, r % 2
    partner = (r + 1 - 2 * core, c)

    across = r + 2 - 4 * y_lo
    edge_to = (across, lax.rem(c + 1 - 2 * core + GROUP, GROUP))
    edge_from = (across, lax.rem(c - 1 + 2 * core + GROUP, GROUP))

    barrier = pltpu.get_barrier_semaphore()
    peers = [(r, lax.rem(c + step, GROUP)) for step in range(1, GROUP)]
    peers += [partner, edge_to, edge_from]
    for peer in peers:
        pl.semaphore_signal(barrier, inc=1, device_id=peer, device_id_type=MESH)
    taps_copy = pltpu.make_async_copy(taps_far, taps, local_sem.at[1])
    taps_copy.start()

    def widen(k, carry):
        at = pl.multiple_of(k * 16, 16)
        staged[pl.ds(pl.multiple_of(k * 256, 256), 256)] = (
            homologs[pl.ds(at, 16)].astype(F32).reshape(256, 128)
        )
        return carry

    lax.fori_loop(0, 16, widen, 0)

    def turn(k, carry):
        for a in range(2):
            trait = 2 * k + a
            flat = staged[pl.ds(trait, SEQS, stride=TRAITS)]
            cols_got[trait, HALO : HALO + COLS] = flat.T.astype(BF16)
        return carry

    lax.fori_loop(0, TRAITS // 2, turn, 0)
    pl.semaphore_wait(barrier, len(peers))

    first = -HALO + 64 * (y_lo + core)

    def block_at(k):
        return BLOCKS - 1 - k + core * (2 * k + 1 - BLOCKS)

    def source_of(k):
        start = first + BLOCK * block_at(k) + COLS
        return lax.rem(plane + start // COLS - 1 + GROUP, GROUP), lax.rem(start, COLS)

    def piece_at(k, place):
        _, start = source_of(k)
        return cols_got.at[
            pl.ds(SHARE * place, SHARE), pl.ds(pl.multiple_of(HALO + start, BLOCK), BLOCK)
        ]

    def slot_of(k, place):
        return rows_got.at[
            pl.ds(SHARE * place, SHARE), pl.ds(pl.multiple_of(BLOCK * block_at(k), BLOCK), BLOCK)
        ]

    def place_at(step):
        return lax.rem(c + step + GROUP, GROUP)

    def scatter_copy(k, step):
        return pltpu.make_async_remote_copy(
            src_ref=piece_at(k, place_at(step)),
            dst_ref=slot_of(k, place_at(step)),
            send_sem=scatter_send.at[k, step],
            recv_sem=scatter_recv.at[k],
            device_id=(r, place_at(step)),
            device_id_type=MESH,
        )

    def own_copy(k):
        return pltpu.make_async_copy(piece_at(k, c), slot_of(k, c), local_sem.at[2 + k])

    def mate_of(place):
        return place + 1 - 2 * lax.rem(place, 2)

    def gather_copy(k, hop, arriving=False):
        ahead = 2 * ((hop - 1) % 3 + 1)
        to = mate_of(c) if hop == 0 else place_at(ahead)
        sent = mate_of(c) if hop > 3 else c
        got = sent
        if arriving:
            got = mate_of(c) if hop == 0 else place_at(-ahead)
            got = mate_of(got) if hop > 3 else got
        return pltpu.make_async_remote_copy(
            src_ref=slot_of(k, sent),
            dst_ref=slot_of(k, got),
            send_sem=gather_send.at[k, hop],
            recv_sem=gather_recv.at[k, hop],
            device_id=(r, to),
            device_id_type=MESH,
        )

    for k in range(BLOCKS):

        @pl.when(source_of(k)[0] == c)
        def _():
            own_copy(k).start()
            for step in range(1, GROUP):
                scatter_copy(k, step).start()

    side = pl.multiple_of((HALO + COLS) * core, HALO)
    edge_copy = pltpu.make_async_remote_copy(
        src_ref=cols_got.at[:, pl.ds(pl.multiple_of(COLS - (COLS - HALO) * core, HALO), HALO)],
        dst_ref=cols_got.at[:, pl.ds(side, HALO)],
        send_sem=edge_send.at[0],
        recv_sem=edge_recv.at[0],
        device_id=edge_to,
        device_id_type=MESH,
    )
    edge_copy.start()
    other_copy = pltpu.make_async_remote_copy(
        src_ref=cols_got.at[:, pl.ds(side, HALO)],
        dst_ref=cols_got.at[:, pl.ds(side, HALO)],
        send_sem=edge_send.at[1],
        recv_sem=edge_recv.at[1],
        device_id=partner,
        device_id_type=MESH,
    )

    def prepare(conv, carry):
        for q in range(3):
            g0 = taps[conv, 0, q].astype(F32)
            g1 = taps[conv, 1, q].astype(F32)
            g2 = taps[conv, 2, q].astype(F32)
            outer, inner = (g0 + g2) * 0.5, g1 * 0.5
            at = (pl.ds(128 * (q // 2), 128), pl.ds(128 * (1 if q == 0 else 0), 128))
            for m, v in enumerate((g0, outer + inner, outer - inner, g2)):
                weights[conv, m, at[0], at[1]] = v.astype(BF16)
        for m in range(4):
            weights[conv, m, 128:, 128:] = jnp.zeros((128, 128), BF16)
        return carry

    taps_copy.wait()
    lax.fori_loop(0, 8, prepare, 0)
    full = pairing[...].astype(F32)
    full = (full - jnp.mean(full, axis=-1, keepdims=True)).astype(BF16)
    to = lax.broadcasted_iota(jnp.int32, (256, 256), 0)
    at = lax.broadcasted_iota(jnp.int32, (256, 256), 1)
    order = jnp.where(at == lax.rem(to, TRAITS) * TRAITS + to // TRAITS, 1.0, 0.0).astype(BF16)
    centred[...] = jnp.dot(order, full, preferred_element_type=F32).T.astype(BF16)
    same = lax.broadcasted_iota(jnp.int32, (64, 64), 0) == lax.broadcasted_iota(
        jnp.int32, (64, 64), 1
    )
    bias = jnp.sum(jnp.where(same, offset[...], 0.0), axis=1, keepdims=True)
    place = lax.broadcasted_iota(jnp.int32, (WIDE, 128), 0) + (c * COLS - HALO)
    inside = jnp.logical_and(place >= 0, place < COLS * GROUP)
    masks[0] = jnp.zeros((WIDE, 128), F32)
    masks[1] = jnp.where(inside, 1.0, 0.0).astype(F32)
    edge_row = jnp.where(jnp.logical_or(r == 0, r == 31), 30, -DEPTH)

    def mask_of(row):
        return masks[jnp.where(row < edge_row, 0, 1)]

    for ref in (map_a, map_a_up, map_b, map_b_up):
        ref[0:OFF] = jnp.zeros((OFF, WIDE, 128), BF16)
    for ref in (products_a, products_b):
        ref[:, :, 0:PAD] = jnp.zeros((4, 2, PAD, 128), F32)
    shift_out[...] = jnp.zeros(shift_out.shape, F32)
    gram[:, :, 128:] = jnp.zeros((BLOCK, TRAITS * TRAITS, 128), BF16)

    for k in range(BLOCKS):

        @pl.when(source_of(k)[0] == c)
        def _():
            own_copy(k).wait()

        @pl.when(source_of(k)[0] != c)
        def _():
            pltpu.make_async_remote_copy(
                src_ref=slot_of(k, c),
                dst_ref=slot_of(k, c),
                send_sem=scatter_send.at[k, 1],
                recv_sem=scatter_recv.at[k],
                device_id=(r, place_at(1)),
                device_id_type=MESH,
            ).wait_recv()

        for hop in range(4):
            gather_copy(k, hop).start()
    for k in range(BLOCKS):
        gather_copy(k, 0, True).wait_recv()
        for hop in range(4, 7):
            gather_copy(k, hop).start()
    edge_copy.wait_recv()
    other_copy.start()

    other_copy.wait()
    edge_copy.wait_send()

    def outer_products():
        for b in range(TRAITS):
            block = lax.dot_general(
                rows_in[...],
                cols_got[b],
                (((1,), (1,)), ((), ())),
                preferred_element_type=F32,
            )
            gram[:, TRAITS * b : TRAITS * (b + 1), :WIDE] = (
                (block * (1.0 / SEQS)).astype(BF16).reshape(BLOCK, TRAITS, WIDE)
            )

    def put(value, row, slot, first_col, width, ahead, target, target_up, whole):
        e = elu(value)
        low, high = HALO - first_col, HALO + COLS - first_col
        if whole:
            e = e * mask_of(row)[first_col : first_col + width]
        else:
            parts = [e[:low] * masks[1, first_col:HALO], e[low : min(high, width)]]
            if width > high:
                parts.append(e[high:] * masks[1, HALO + COLS : first_col + width])
            e = jnp.concatenate(parts, axis=0)
        target[row + OFF, first_col : first_col + width] = e.astype(BF16)
        if ahead == 8:
            moved = jnp.concatenate((e[8:], e[:8]), axis=0)
        else:
            shift_out[slot, 0:width] = e
            moved = shift_out[slot, ahead : ahead + width]
        target_up[row + OFF, first_col : first_col + width] = moved.astype(BF16)

    def row_copies(stage, count, target, target_up):
        return [
            pltpu.make_async_remote_copy(
                src_ref=ref.at[TOP - 1 - t + OFF],
                dst_ref=ref.at[TOP + t + OFF],
                send_sem=row_send.at[stage % 2, which, t],
                recv_sem=row_recv.at[stage % 2, which, t],
                device_id=partner,
                device_id_type=MESH,
            )
            for t in range(count)
            for which, ref in enumerate((target, target_up))
        ]

    def start_all(copies):
        for copy in copies:
            copy.start()

    def wait_all(copies):
        for copy in copies:
            copy.wait()

    def first_rows(k, chunk):
        for slot in range(8):
            index = 8 * chunk + slot
            row = TOP - 1 - BLOCK * k - index
            projected = jnp.dot(
                centred[...],
                gram[BLOCK - 1 - index + core * (2 * index + 1 - BLOCK)],
                preferred_element_type=F32,
            )
            spread = jnp.mean(projected * projected, axis=0, keepdims=True)
            value = (projected[:, :WIDE] * lax.rsqrt(spread + 1e-05)[:, :WIDE]).T
            state[row + XOFF] = value
            put(value, row, 8 * chunk + slot, 0, WIDE, 1, map_a, map_a_up, True)

    for k in range(BLOCKS):
        for hop in range(1, 7):
            gather_copy(k, hop, True).wait_recv()
        rows_at = pl.ds(pl.multiple_of(BLOCK * block_at(k), BLOCK), BLOCK)
        for a in range(TRAITS):
            for half in range(2):
                staged[pl.ds(1024 * half + a, BLOCK, stride=TRAITS)] = rows_got[
                    a, rows_at, 128 * half : 128 * (half + 1)
                ].astype(F32)
        for half in range(2):
            rows_in[:, 128 * half : 128 * (half + 1)] = staged[
                1024 * half : 1024 * half + BLOCK * TRAITS
            ].astype(BF16)
        outer_products()

        for chunk in range(2):
            first_rows(k, chunk)
        if k == 0:
            copies = row_copies(0, 1, map_a, map_a_up)
            start_all(copies)
    for k in range(BLOCKS):
        for hop in range(7):
            gather_copy(k, hop).wait_send()

        @pl.when(source_of(k)[0] == c)
        def _():
            for step in range(1, GROUP):
                scatter_copy(k, step).wait_send()

    def maps_of(stage):
        pair = ((map_a, map_a_up), (map_b, map_b_up))
        return pair[stage % 2], pair[1 - stage % 2]

    def multiply(item, m, held):
        stage, base, depth = item
        d, _, col, width = STAGES[stage]
        span = slice(col, col + width)
        low, high, sign = ((0, 2, -1), (1, 2, 1), (2, 1, -1), (1, 3, -1))[m]

        def lines(ref, at):
            parts = [
                ref[base + OFF + 2 * d * k + at : base + OFF + 2 * d * k + at + d, span]
                for k in range(depth // (2 * d))
            ]
            return parts[0] if len(parts) == 1 else jnp.concatenate(parts, axis=0)

        sides = []
        for ref in maps_of(stage)[0]:
            x, y = lines(ref, (low - 1) * d), lines(ref, (high - 1) * d)
            sides.append(x + y if sign > 0 else x - y)
        count = depth // 2 * width
        tap = m if m in (1, 2) else (3 * core if m == 0 else 3 - 3 * core)
        product = jnp.dot(
            jnp.concatenate(sides, axis=-1).reshape(count, 256),
            weights[stage, tap],
            preferred_element_type=F32,
        )
        held[m, 0, PAD : PAD + count] = product[:, :128]
        held[m, 1, PAD : PAD + count] = product[:, 128:]

    def finish(item, pairs, held):
        stage, base, depth = item
        d, _, col, width = STAGES[stage]
        residual, last = stage % 2 == 1, stage == len(STAGES) - 1
        target, target_up = maps_of(stage)[1]
        span = slice(col, col + width)
        for p in pairs:
            block, t = p // d, p % d
            at = PAD + p * width

            def term(m, at=at):
                return held[m, 0, at : at + width], held[m, 1, at - d : at - d + width]

            (a0, b0), (a1, b1), (a2, b2), (a3, b3) = (term(m) for m in range(4))
            upper = (a0 + b0) + (a1 + b1) + (a2 + b2)
            lower = (a1 + b1) - (a2 + b2) - (a3 + b3)
            for half, conv in enumerate((upper, lower)):
                row = base + 2 * d * block + d * half + t
                if residual:
                    conv = conv + state[row + XOFF, span]
                    if not last:
                        state[row + XOFF, span] = conv
                if last:
                    final = elu(conv[16:144]).astype(BF16)
                    logits = lax.dot_general(
                        classes[...],
                        final,
                        (((1,), (1,)), ((), ())),
                        preferred_element_type=F32,
                    )
                    own = row - 30
                    out[own + core * (31 - 2 * own)] = (logits + bias).astype(BF16)
                else:
                    ahead = STAGES[stage + 1][0]
                    slot = 2 * p + half
                    put(conv, row, slot, col, width, ahead, target, target_up, row < 30)

    items = []
    for stage, (_, depths, _, _) in enumerate(STAGES):
        base = TOP
        for depth in depths:
            base -= depth
            items.append((stage, base, depth))

    done, held_done = None, None
    for step, item in enumerate(items + [None]):
        held = (products_a, products_b)[step % 2]
        if item is not None and item[1] + item[2] == TOP:
            wait_all(copies)
        for m in range(4):
            if item is not None:
                multiply(item, m, held)
            if done is not None:
                pairs = done[2] // 2
                finish(done, range(pairs * m // 4, pairs * (m + 1) // 4), held_done)
        if done is not None and done[1] + done[2] == TOP and done[0] + 1 < len(STAGES):
            copies = row_copies(done[0] + 1, STAGES[done[0] + 1][0], *maps_of(done[0])[1])
            start_all(copies)
        done, held_done = item, held


def body(homologs, pairing, taps, classes, offset):
    homologs = jnp.transpose(homologs, (0, 2, 1))
    taps = taps.reshape(8, 3, 3, 128, 128)
    vmem = pl.BlockSpec(memory_space=pltpu.VMEM)
    far = pl.BlockSpec(memory_space=pl.ANY)
    out = pl.pallas_call(
        kernel,
        out_shape=jax.ShapeDtypeStruct((ROWS, 64, COLS), BF16),
        in_specs=[vmem, vmem, far, vmem, vmem],
        out_specs=vmem,
        scratch_shapes=[
            pltpu.VMEM((SEQS * TRAITS, 128), F32),
            pltpu.VMEM((TRAITS, 64, SEQS), BF16),
            pltpu.VMEM((BLOCK * TRAITS, SEQS), BF16),
            pltpu.VMEM((TRAITS, WIDE, SEQS), BF16),
            pltpu.VMEM((BLOCK, TRAITS * TRAITS, 256), BF16),
            pltpu.VMEM((8, 4, 256, 256), BF16),
            pltpu.VMEM((64, WIDE, 128), F32),
            pltpu.VMEM((DEPTH, WIDE, 128), BF16),
            pltpu.VMEM((DEPTH, WIDE, 128), BF16),
            pltpu.VMEM((DEPTH, WIDE, 128), BF16),
            pltpu.VMEM((DEPTH, WIDE, 128), BF16),
            pltpu.VMEM((4, 2, PAD + 8 * WIDE, 128), F32),
            pltpu.VMEM((4, 2, PAD + 8 * WIDE, 128), F32),
            pltpu.VMEM((16, WIDE + PAD, 128), F32),
            pltpu.VMEM((2, WIDE, 128), F32),
            pltpu.VMEM((8, 3, 3, 128, 128), BF16),
            pltpu.VMEM((128, 256), BF16),
            pltpu.SemaphoreType.DMA((2 + BLOCKS,)),
            pltpu.SemaphoreType.DMA((BLOCKS, GROUP)),
            pltpu.SemaphoreType.DMA((BLOCKS,)),
            pltpu.SemaphoreType.DMA((BLOCKS, GROUP)),
            pltpu.SemaphoreType.DMA((BLOCKS, GROUP)),
            pltpu.SemaphoreType.DMA((2,)),
            pltpu.SemaphoreType.DMA((2,)),
            pltpu.SemaphoreType.DMA((2, 2, 8)),
            pltpu.SemaphoreType.DMA((2, 2, 8)),
        ],
        compiler_params=pltpu.CompilerParams(
            collective_id=0, has_side_effects=True, vmem_limit_bytes=60 * 2**20
        ),
        name="distogram",
    )(homologs, pairing, taps, classes.T, offset.reshape(1, 64))
    return jnp.transpose(out, (0, 2, 1))


def solution(mesh):
    placed = (P(None, "col", None), P(), P(), P(), P())
    return jax.shard_map(
        body, mesh=mesh, in_specs=placed, out_specs=P("row", "col", None), check_vma=False
    )
```

```python
import functools

import jax
import jax.numpy as jnp
from jax import lax
from jax.experimental import pallas as pl
from jax.experimental.pallas import tpu as pltpu
from jax.sharding import PartitionSpec as P

MESH = pl.DeviceIdType.MESH
F32, BF16 = jnp.float32, jnp.bfloat16

ROWS = 32
COLS = 128
HALO = 32
WIDE = COLS + 2 * HALO
TRAITS = 16
SEQS = 256
BLOCK = 16
BLOCKS = 4
SHARE = 2
GROUP = 8
OFF = 4
XOFF = 2
TOP = 62
DEPTH = 74
PAD = 8

STAGES = (
    (1, (16, 16, 16, 14), 0, 192),
    (1, (16, 16, 16, 12), 0, 192),
    (2, (16, 16, 16, 12), 0, 192),
    (2, (16, 16, 12, 12), 0, 192),
    (4, (16, 16, 16, 8), 0, 192),
    (4, (16, 16, 16), 0, 176),
    (8, (16, 16, 16), 16, 160),
    (8, (16, 16), 16, 144),
)


def elu(v):
    return jnp.maximum(v, jnp.exp(jnp.minimum(v, 0.0)) - 1.0)


def kernel(
    homologs,
    pairing,
    taps_far,
    classes,
    offset,
    out,
    staged,
    rows_got,
    rows_in,
    cols_got,
    gram,
    weights,
    state,
    map_a,
    map_a_up,
    map_b,
    map_b_up,
    products_a,
    products_b,
    shift_out,
    masks,
    taps,
    centred,
    local_sem,
    scatter_send,
    scatter_recv,
    gather_send,
    gather_recv,
    edge_send,
    edge_recv,
    row_send,
    row_recv,
):
    r, c = lax.axis_index("row"), lax.axis_index("col")
    plane, y_lo, core = r // 4, (r // 2) % 2, r % 2
    partner = (r + 1 - 2 * core, c)

    across = r + 2 - 4 * y_lo
    edge_to = (across, lax.rem(c + 1 - 2 * core + GROUP, GROUP))
    edge_from = (across, lax.rem(c - 1 + 2 * core + GROUP, GROUP))

    barrier = pltpu.get_barrier_semaphore()
    peers = [(r, lax.rem(c + step, GROUP)) for step in range(1, GROUP)]
    peers += [partner, edge_to, edge_from]
    for peer in peers:
        pl.semaphore_signal(barrier, inc=1, device_id=peer, device_id_type=MESH)
    taps_copy = pltpu.make_async_copy(taps_far, taps, local_sem.at[1])
    taps_copy.start()

    def widen(k, carry):
        at = pl.multiple_of(k * 16, 16)
        staged[pl.ds(pl.multiple_of(k * 256, 256), 256)] = (
            homologs[pl.ds(at, 16)].astype(F32).reshape(256, 128)
        )
        return carry

    lax.fori_loop(0, 16, widen, 0)

    def turn(k, carry):
        for a in range(2):
            trait = 2 * k + a
            flat = staged[pl.ds(trait, SEQS, stride=TRAITS)]
            cols_got[trait, HALO : HALO + COLS] = flat.T.astype(BF16)
        return carry

    lax.fori_loop(0, TRAITS // 2, turn, 0)
    pl.semaphore_wait(barrier, len(peers))

    first = -HALO + 64 * (y_lo + core)

    def block_at(k):
        return BLOCKS - 1 - k + core * (2 * k + 1 - BLOCKS)

    def source_of(k):
        start = first + BLOCK * block_at(k) + COLS
        return lax.rem(plane + start // COLS - 1 + GROUP, GROUP), lax.rem(start, COLS)

    def piece_at(k, place):
        _, start = source_of(k)
        return cols_got.at[
            pl.ds(SHARE * place, SHARE), pl.ds(pl.multiple_of(HALO + start, BLOCK), BLOCK)
        ]

    def slot_of(k, place):
        return rows_got.at[
            pl.ds(SHARE * place, SHARE), pl.ds(pl.multiple_of(BLOCK * block_at(k), BLOCK), BLOCK)
        ]

    def place_at(step):
        return lax.rem(c + step + GROUP, GROUP)

    def scatter_copy(k, step):
        return pltpu.make_async_remote_copy(
            src_ref=piece_at(k, place_at(step)),
            dst_ref=slot_of(k, place_at(step)),
            send_sem=scatter_send.at[k, step],
            recv_sem=scatter_recv.at[k],
            device_id=(r, place_at(step)),
            device_id_type=MESH,
        )

    def own_copy(k):
        return pltpu.make_async_copy(piece_at(k, c), slot_of(k, c), local_sem.at[2 + k])

    def mate_of(place):
        return place + 1 - 2 * lax.rem(place, 2)

    def gather_copy(k, hop, arriving=False):
        ahead = 2 * ((hop - 1) % 3 + 1)
        to = mate_of(c) if hop == 0 else place_at(ahead)
        sent = mate_of(c) if hop > 3 else c
        got = sent
        if arriving:
            got = mate_of(c) if hop == 0 else place_at(-ahead)
            got = mate_of(got) if hop > 3 else got
        return pltpu.make_async_remote_copy(
            src_ref=slot_of(k, sent),
            dst_ref=slot_of(k, got),
            send_sem=gather_send.at[k, hop],
            recv_sem=gather_recv.at[k, hop],
            device_id=(r, to),
            device_id_type=MESH,
        )

    for k in range(BLOCKS):

        @pl.when(source_of(k)[0] == c)
        def _():
            own_copy(k).start()
            for step in range(1, GROUP):
                scatter_copy(k, step).start()

    side = pl.multiple_of((HALO + COLS) * core, HALO)
    edge_copy = pltpu.make_async_remote_copy(
        src_ref=cols_got.at[:, pl.ds(pl.multiple_of(COLS - (COLS - HALO) * core, HALO), HALO)],
        dst_ref=cols_got.at[:, pl.ds(side, HALO)],
        send_sem=edge_send.at[0],
        recv_sem=edge_recv.at[0],
        device_id=edge_to,
        device_id_type=MESH,
    )
    edge_copy.start()
    other_copy = pltpu.make_async_remote_copy(
        src_ref=cols_got.at[:, pl.ds(side, HALO)],
        dst_ref=cols_got.at[:, pl.ds(side, HALO)],
        send_sem=edge_send.at[1],
        recv_sem=edge_recv.at[1],
        device_id=partner,
        device_id_type=MESH,
    )

    def prepare(conv, carry):
        for q in range(3):
            g0 = taps[conv, 0, q].astype(F32)
            g1 = taps[conv, 1, q].astype(F32)
            g2 = taps[conv, 2, q].astype(F32)
            outer, inner = (g0 + g2) * 0.5, g1 * 0.5
            at = (pl.ds(128 * (q // 2), 128), pl.ds(128 * (1 if q == 0 else 0), 128))
            for m, v in enumerate((g0, outer + inner, outer - inner, g2)):
                weights[conv, m, at[0], at[1]] = v.astype(BF16)
        for m in range(4):
            weights[conv, m, 128:, 128:] = jnp.zeros((128, 128), BF16)
        return carry

    taps_copy.wait()
    lax.fori_loop(0, 8, prepare, 0)
    full = pairing[...].astype(F32)
    full = (full - jnp.mean(full, axis=-1, keepdims=True)).astype(BF16)
    to = lax.broadcasted_iota(jnp.int32, (256, 256), 0)
    at = lax.broadcasted_iota(jnp.int32, (256, 256), 1)
    order = jnp.where(at == lax.rem(to, TRAITS) * TRAITS + to // TRAITS, 1.0, 0.0).astype(BF16)
    centred[...] = jnp.dot(order, full, preferred_element_type=F32).T.astype(BF16)
    same = lax.broadcasted_iota(jnp.int32, (64, 64), 0) == lax.broadcasted_iota(
        jnp.int32, (64, 64), 1
    )
    bias = jnp.sum(jnp.where(same, offset[...], 0.0), axis=1, keepdims=True)
    place = lax.broadcasted_iota(jnp.int32, (WIDE, 128), 0) + (c * COLS - HALO)
    inside = jnp.logical_and(place >= 0, place < COLS * GROUP)
    masks[0] = jnp.zeros((WIDE, 128), F32)
    masks[1] = jnp.where(inside, 1.0, 0.0).astype(F32)
    edge_row = jnp.where(jnp.logical_or(r == 0, r == 31), 30, -DEPTH)

    def mask_of(row):
        return masks[jnp.where(row < edge_row, 0, 1)]

    for ref in (map_a, map_a_up, map_b, map_b_up):
        ref[0:OFF] = jnp.zeros((OFF, WIDE, 128), BF16)
    for ref in (products_a, products_b):
        ref[:, :, 0:PAD] = jnp.zeros((4, 2, PAD, 128), F32)
    shift_out[...] = jnp.zeros(shift_out.shape, F32)
    gram[:, :, 128:] = jnp.zeros((BLOCK, TRAITS * TRAITS, 128), BF16)

    for k in range(BLOCKS):

        @pl.when(source_of(k)[0] == c)
        def _():
            own_copy(k).wait()

        @pl.when(source_of(k)[0] != c)
        def _():
            pltpu.make_async_remote_copy(
                src_ref=slot_of(k, c),
                dst_ref=slot_of(k, c),
                send_sem=scatter_send.at[k, 1],
                recv_sem=scatter_recv.at[k],
                device_id=(r, place_at(1)),
                device_id_type=MESH,
            ).wait_recv()

        for hop in range(4):
            gather_copy(k, hop).start()
    for k in range(BLOCKS):
        gather_copy(k, 0, True).wait_recv()
        for hop in range(4, 7):
            gather_copy(k, hop).start()
    edge_copy.wait_recv()
    other_copy.start()

    other_copy.wait()
    edge_copy.wait_send()

    def outer_products():
        for b in range(TRAITS):
            block = lax.dot_general(
                rows_in[...],
                cols_got[b],
                (((1,), (1,)), ((), ())),
                preferred_element_type=F32,
            )
            gram[:, TRAITS * b : TRAITS * (b + 1), :WIDE] = (
                (block * (1.0 / SEQS)).astype(BF16).reshape(BLOCK, TRAITS, WIDE)
            )

    def put(value, row, slot, first_col, width, ahead, target, target_up, whole):
        e = elu(value)
        low, high = HALO - first_col, HALO + COLS - first_col
        if whole:
            e = e * mask_of(row)[first_col : first_col + width]
        else:
            parts = [e[:low] * masks[1, first_col:HALO], e[low : min(high, width)]]
            if width > high:
                parts.append(e[high:] * masks[1, HALO + COLS : first_col + width])
            e = jnp.concatenate(parts, axis=0)
        target[row + OFF, first_col : first_col + width] = e.astype(BF16)
        if ahead == 8:
            moved = jnp.concatenate((e[8:], e[:8]), axis=0)
        else:
            shift_out[slot, 0:width] = e
            moved = shift_out[slot, ahead : ahead + width]
        target_up[row + OFF, first_col : first_col + width] = moved.astype(BF16)

    def row_copies(stage, count, target, target_up):
        return [
            pltpu.make_async_remote_copy(
                src_ref=ref.at[TOP - 1 - t + OFF],
                dst_ref=ref.at[TOP + t + OFF],
                send_sem=row_send.at[stage % 2, which, t],
                recv_sem=row_recv.at[stage % 2, which, t],
                device_id=partner,
                device_id_type=MESH,
            )
            for t in range(count)
            for which, ref in enumerate((target, target_up))
        ]

    def start_all(copies):
        for copy in copies:
            copy.start()

    def wait_all(copies):
        for copy in copies:
            copy.wait()

    def first_rows(k, chunk):
        for slot in range(8):
            index = 8 * chunk + slot
            row = TOP - 1 - BLOCK * k - index
            projected = jnp.dot(
                centred[...],
                gram[BLOCK - 1 - index + core * (2 * index + 1 - BLOCK)],
                preferred_element_type=F32,
            )
            spread = jnp.mean(projected * projected, axis=0, keepdims=True)
            value = (projected[:, :WIDE] * lax.rsqrt(spread + 1e-05)[:, :WIDE]).T
            state[row + XOFF] = value
            put(value, row, 8 * chunk + slot, 0, WIDE, 1, map_a, map_a_up, True)

    copies = row_copies(0, 1, map_a, map_a_up)

    def block_rows(k, carry):
        for hop in range(1, 7):
            gather_copy(k, hop, True).wait_recv()
        rows_at = pl.ds(pl.multiple_of(BLOCK * block_at(k), BLOCK), BLOCK)
        for a in range(TRAITS):
            for half in range(2):
                staged[pl.ds(1024 * half + a, BLOCK, stride=TRAITS)] = rows_got[
                    a, rows_at, 128 * half : 128 * (half + 1)
                ].astype(F32)
        for half in range(2):
            rows_in[:, 128 * half : 128 * (half + 1)] = staged[
                1024 * half : 1024 * half + BLOCK * TRAITS
            ].astype(BF16)
        outer_products()

        for chunk in range(2):
            first_rows(k, chunk)

        @pl.when(k == 0)
        def _():
            start_all(copies)

        return carry

    lax.fori_loop(0, BLOCKS, block_rows, 0)
    for k in range(BLOCKS):
        for hop in range(7):
            gather_copy(k, hop).wait_send()

        @pl.when(source_of(k)[0] == c)
        def _():
            for step in range(1, GROUP):
                scatter_copy(k, step).wait_send()

    def maps_of(stage):
        pair = ((map_a, map_a_up), (map_b, map_b_up))
        return pair[stage % 2], pair[1 - stage % 2]

    def multiply(item, m, held):
        stage, base, depth = item
        d, _, col, width = STAGES[stage]
        span = slice(col, col + width)
        low, high, sign = ((0, 2, -1), (1, 2, 1), (2, 1, -1), (1, 3, -1))[m]

        def lines(ref, at):
            parts = [
                ref[base + OFF + 2 * d * k + at : base + OFF + 2 * d * k + at + d, span]
                for k in range(depth // (2 * d))
            ]
            return parts[0] if len(parts) == 1 else jnp.concatenate(parts, axis=0)

        sides = []
        for ref in maps_of(stage)[0]:
            x, y = lines(ref, (low - 1) * d), lines(ref, (high - 1) * d)
            sides.append(x + y if sign > 0 else x - y)
        count = depth // 2 * width
        tap = m if m in (1, 2) else (3 * core if m == 0 else 3 - 3 * core)
        product = jnp.dot(
            jnp.concatenate(sides, axis=-1).reshape(count, 256),
            weights[stage, tap],
            preferred_element_type=F32,
        )
        held[m, 0, PAD : PAD + count] = product[:, :128]
        held[m, 1, PAD : PAD + count] = product[:, 128:]

    def finish(item, pairs, held):
        stage, base, depth = item
        d, _, col, width = STAGES[stage]
        residual, last = stage % 2 == 1, stage == len(STAGES) - 1
        target, target_up = maps_of(stage)[1]
        span = slice(col, col + width)
        for p in pairs:
            block, t = p // d, p % d
            at = PAD + p * width

            def term(m, at=at):
                return held[m, 0, at : at + width], held[m, 1, at - d : at - d + width]

            (a0, b0), (a1, b1), (a2, b2), (a3, b3) = (term(m) for m in range(4))
            upper = (a0 + b0) + (a1 + b1) + (a2 + b2)
            lower = (a1 + b1) - (a2 + b2) - (a3 + b3)
            for half, conv in enumerate((upper, lower)):
                row = base + 2 * d * block + d * half + t
                if residual:
                    conv = conv + state[row + XOFF, span]
                    if not last:
                        state[row + XOFF, span] = conv
                if last:
                    final = elu(conv[16:144]).astype(BF16)
                    logits = lax.dot_general(
                        classes[...],
                        final,
                        (((1,), (1,)), ((), ())),
                        preferred_element_type=F32,
                    )
                    own = row - 30
                    out[own + core * (31 - 2 * own)] = (logits + bias).astype(BF16)
                else:
                    ahead = STAGES[stage + 1][0]
                    slot = 2 * p + half
                    put(conv, row, slot, col, width, ahead, target, target_up, row < 30)

    items = []
    for stage, (_, depths, _, _) in enumerate(STAGES):
        base = TOP
        for depth in depths:
            base -= depth
            items.append((stage, base, depth))

    done, held_done = None, None
    for step, item in enumerate(items + [None]):
        held = (products_a, products_b)[step % 2]
        if item is not None and item[1] + item[2] == TOP:
            wait_all(copies)
        for m in range(4):
            if item is not None:
                multiply(item, m, held)
            if done is not None:
                pairs = done[2] // 2
                finish(done, range(pairs * m // 4, pairs * (m + 1) // 4), held_done)
        if done is not None and done[1] + done[2] == TOP and done[0] + 1 < len(STAGES):
            copies = row_copies(done[0] + 1, STAGES[done[0] + 1][0], *maps_of(done[0])[1])
            start_all(copies)
        done, held_done = item, held


def body(homologs, pairing, taps, classes, offset):
    homologs = jnp.transpose(homologs, (0, 2, 1))
    taps = taps.reshape(8, 3, 3, 128, 128)
    vmem = pl.BlockSpec(memory_space=pltpu.VMEM)
    far = pl.BlockSpec(memory_space=pl.ANY)
    out = pl.pallas_call(
        kernel,
        out_shape=jax.ShapeDtypeStruct((ROWS, 64, COLS), BF16),
        in_specs=[vmem, vmem, far, vmem, vmem],
        out_specs=vmem,
        scratch_shapes=[
            pltpu.VMEM((SEQS * TRAITS, 128), F32),
            pltpu.VMEM((TRAITS, 64, SEQS), BF16),
            pltpu.VMEM((BLOCK * TRAITS, SEQS), BF16),
            pltpu.VMEM((TRAITS, WIDE, SEQS), BF16),
            pltpu.VMEM((BLOCK, TRAITS * TRAITS, 256), BF16),
            pltpu.VMEM((8, 4, 256, 256), BF16),
            pltpu.VMEM((64, WIDE, 128), F32),
            pltpu.VMEM((DEPTH, WIDE, 128), BF16),
            pltpu.VMEM((DEPTH, WIDE, 128), BF16),
            pltpu.VMEM((DEPTH, WIDE, 128), BF16),
            pltpu.VMEM((DEPTH, WIDE, 128), BF16),
            pltpu.VMEM((4, 2, PAD + 8 * WIDE, 128), F32),
            pltpu.VMEM((4, 2, PAD + 8 * WIDE, 128), F32),
            pltpu.VMEM((16, WIDE + PAD, 128), F32),
            pltpu.VMEM((2, WIDE, 128), F32),
            pltpu.VMEM((8, 3, 3, 128, 128), BF16),
            pltpu.VMEM((128, 256), BF16),
            pltpu.SemaphoreType.DMA((2 + BLOCKS,)),
            pltpu.SemaphoreType.DMA((BLOCKS, GROUP)),
            pltpu.SemaphoreType.DMA((BLOCKS,)),
            pltpu.SemaphoreType.DMA((BLOCKS, GROUP)),
            pltpu.SemaphoreType.DMA((BLOCKS, GROUP)),
            pltpu.SemaphoreType.DMA((2,)),
            pltpu.SemaphoreType.DMA((2,)),
            pltpu.SemaphoreType.DMA((2, 2, 8)),
            pltpu.SemaphoreType.DMA((2, 2, 8)),
        ],
        compiler_params=pltpu.CompilerParams(
            collective_id=0, has_side_effects=True, vmem_limit_bytes=60 * 2**20
        ),
        name="distogram",
    )(homologs, pairing, taps, classes.T, offset.reshape(1, 64))
    return jnp.transpose(out, (0, 2, 1))


def solution(mesh):
    placed = (P(None, "col", None), P(), P(), P(), P())
    return jax.shard_map(
        body, mesh=mesh, in_specs=placed, out_specs=P("row", "col", None), check_vma=False
    )
```
